32 devices in a mesh: vol: 4 (over y, core), sec: 8 (over z, x).
Axes of the slice: x: 2, y: 2, z: 4, core: 2. Of those that a mesh axis runs over, the one named last changes fastest.
Arguments:
- rhs: float32 [64, 8, 64, 1024], P(None, None, 'vol', 'sec'), may hold values from -6 to 6
- flux_in: float32 [64, 64, 1024], P(None, 'vol', 'sec'), may hold values from -12 to 12
- materials: int32 [8, 64, 1024], P(None, 'vol', 'sec'), may hold values from 0 to 7
- mat_coef: float32 [8], replicated, may hold values from 0.5 to 4
- owner_perm: int32 [8], replicated, may hold values from 0 to 7, each once
- blocks: bfloat16 [8, 8192, 8192], P('sec', None, 'vol'), may hold values from -0.0625 to 0.0625
Outputs:
- solution: float32 [64, 8, 64, 1024], P(None, None, 'vol', 'sec')
- flux_out: float32 [64, 64, 1024], P(None, 'vol', 'sec')
The draws below stay inside these ranges and needn't reach their ends.
Inputs may be any that keep to these rules, and one draw needn't show every extreme that they name: `owner_perm`: every harmonic index appears once.
All inputs are finite; a program needn't handle non-finite values.
Results may differ from the reference program's by a relative error of at most 0.008.
Values may be sent and summed in bfloat16 or wider, within the bound.
A program may use at most 128 MiB of HBM per device.

```python
import math
import jax
import jax.numpy as jnp
from jax import lax

ORDER = 8192
PTS = 128
EXC = 64
DEPTH = 8
SWEEPS = 4
NMAT = 8
SECTORS = 8
NZ = 64
NA = 1024


def place_ends(values, rng, smallest, top_value):
    longest = values.shape.index(max(values.shape))
    spots = []
    for shift in (0, 1):
        where = [jax.random.randint(jax.random.fold_in(rng, axis), (), 0, length) for axis, length in enumerate(values.shape)]
        where[longest] = (where[longest] + shift) % values.shape[longest]
        spots.append(tuple(where))
    return values.at[spots[0]].set(smallest).at[spots[1]].set(top_value)


def shard_levels(own_key, shape, cuts, smallest, largest):
    def one(dim, parts):
        heights = jax.random.uniform(jax.random.fold_in(jax.random.fold_in(own_key, 6), dim), (parts,), jnp.float32, smallest / len(cuts), largest / len(cuts))
        return jnp.repeat(jnp.exp(heights), shape[dim] // parts).reshape((-1,) + (1,) * (len(shape) - dim - 1))

    factor_of = one(*cuts[0])
    for cut in cuts[1:]:
        factor_of = factor_of * one(*cut)
    return factor_of


def gaussian(own_key, extent, width, reach, split=(), held_as=jnp.bfloat16):
    values = jax.random.normal(own_key, extent, jnp.float32) * width
    if len(split) > 0:
        values = shard_levels(own_key, extent, split, -0.22, 0.18) * values
    return jnp.clip(values, min=-reach, max=reach).astype(held_as)


def setup_inputs(seed: int = 0) -> dict:
    key_of = jax.random.split(jax.random.key(seed), 7)
    rhs = gaussian(key_of[0], (EXC, DEPTH, NZ, NA), 1.0, 6.0, ((2, 4), (3, 8)), jnp.float32)
    flux_in = gaussian(key_of[1], (EXC, NZ, NA), 2.0, 12.0, ((1, 4), (2, 8)), jnp.float32)
    materials = place_ends(jax.random.randint(key_of[2], (DEPTH, NZ, NA), 0, NMAT), jax.random.fold_in(key_of[2], 1), 0, NMAT - 1).astype(jnp.int32)
    mat_coef = jnp.clip(jnp.exp(jax.random.uniform(key_of[3], (NMAT,), jnp.float32, math.log(0.5), math.log(4.0))), 0.5, 4.0)
    owner_perm = jax.random.permutation(key_of[4], SECTORS).astype(jnp.int32)
    blocks = gaussian(key_of[5], (SECTORS, ORDER, ORDER), ORDER ** -0.5, 0.0625, ((0, 8), (2, 4)))
    return {"rhs": rhs, "flux_in": flux_in, "materials": materials, "mat_coef": mat_coef, "owner_perm": owner_perm, "blocks": blocks}


center = 1.0
radius = 0.93

def harmonic_basis(harmonic_ids, sector_ids, sector_count):
    midpoint = sector_count // 2
    wavenum = jnp.where(harmonic_ids <= midpoint, harmonic_ids, harmonic_ids - midpoint)
    phases = 2.0 * jnp.pi * (wavenum * sector_ids % sector_count).astype(jnp.float32) / sector_count
    basis_value = jnp.where(harmonic_ids <= midpoint, jnp.cos(phases), jnp.sin(phases))
    endpoint = (harmonic_ids == 0) | (harmonic_ids == midpoint)
    weight_scale = jnp.where(endpoint, math.sqrt(1.0 / sector_count), math.sqrt(2.0 / sector_count))
    return (basis_value * weight_scale).astype(jnp.float32)

def neighbour_total(values):
    depth_pad = jnp.pad(values, ((0, 0), (1, 1), (0, 0), (0, 0)))
    total = depth_pad[:, 2:] + depth_pad[:, :-2]
    total = total + jnp.roll(values, 1, 2) + jnp.roll(values, -1, 2)
    total = total + jnp.roll(values, 1, 3) + jnp.roll(values, -1, 3)
    return total

def apply_block(operands):
    vector, matrix = operands
    return jnp.dot(vector.astype(jnp.float32), matrix.astype(jnp.float32), preferred_element_type=jnp.float32)

def reference(rhs, flux_in, materials, mat_coef, owner_perm, blocks):
    onehot = (materials[..., None] == jnp.arange(NMAT, dtype=jnp.int32)).astype(jnp.float32)
    sigma = lax.optimization_barrier(jnp.sum(onehot * mat_coef, -1))
    diagonal = 6.0 + sigma
    inverse = 1.0 / diagonal
    source = rhs.at[:, DEPTH - 1].add(flux_in)
    sigma_one = center / radius
    solution = jnp.zeros_like(rhs)
    remainder = source
    direction = remainder * inverse / center
    ratio_now = 1.0 / sigma_one
    for sweep in range(SWEEPS):
        solution = solution + direction
        if sweep + 1 < SWEEPS:
            remainder = remainder - (diagonal * direction - neighbour_total(direction))
            ratio_next = 1.0 / (2.0 * sigma_one - ratio_now)
            direction = ratio_next * ratio_now * direction + 2.0 * ratio_next / radius * remainder * inverse
            ratio_now = ratio_next
    traces = solution[:, DEPTH - 1].astype(jnp.bfloat16).reshape(EXC, NZ, SECTORS, PTS).astype(jnp.float32)
    basis = harmonic_basis(owner_perm[:, None], jnp.arange(SECTORS, dtype=jnp.int32)[None, :], SECTORS)
    harmonics = jnp.einsum('ds,ezsp->dezp', basis, traces, precision=lax.Precision.HIGHEST)
    harmonics = harmonics.reshape(SECTORS, EXC, ORDER).astype(jnp.bfloat16)
    response = lax.map(apply_block, (harmonics, blocks))
    response = response.reshape(SECTORS, EXC, NZ, PTS)
    flux_out = jnp.einsum('ds,dezp->ezsp', basis, response, precision=lax.Precision.HIGHEST)
    return (solution, flux_out.reshape(EXC, NZ, SECTORS * PTS))
```

```python
import functools
import math

import jax
import jax.numpy as jnp
import numpy as np
from jax import lax
from jax.experimental import pallas as pl
from jax.experimental.pallas import tpu as pltpu
from jax.sharding import PartitionSpec as P

SWEEPS = 4
HALVES = 2
CHUNK = 16
GROUP = 4
MESH = pl.DeviceIdType.MESH
F32, BF16 = jnp.float32, jnp.bfloat16

center = 1.0
radius = 0.93


def basis_table(count):
    harm = np.arange(count)[:, None]
    sect = np.arange(count)[None, :]
    mid = count // 2
    wave = np.where(harm <= mid, harm, harm - mid)
    phase = 2.0 * np.pi * (wave * sect % count) / count
    value = np.where(harm <= mid, np.cos(phase), np.sin(phase))
    ends = (harm == 0) | (harm == mid)
    return (value * np.where(ends, math.sqrt(1.0 / count), math.sqrt(2.0 / count))).astype(np.float32)


def neighbour_matrices(depth, axial, pts):
    rows = depth * axial
    d, z = np.divmod(np.arange(rows), axial)
    same_d = d[:, None] == d[None, :]
    same_z = z[:, None] == z[None, :]
    near = (same_d & (abs(z[:, None] - z[None, :]) == 1)) | (
        same_z & (abs(d[:, None] - d[None, :]) == 1)
    )
    out = np.zeros((2, rows, rows + 4 * depth), np.float32)
    out[:, :, :rows] = near
    for j in range(2):
        for layer in range(depth):
            out[j, layer * axial, rows + j * depth + layer] = 1.0
            out[j, layer * axial + axial - 1, rows + 2 * depth + j * depth + layer] = 1.0
    p = np.arange(pts)
    shift = (abs(p[:, None] - p[None, :]) == 1).astype(np.float32)
    return jnp.asarray(out, BF16), jnp.asarray(shift, BF16)


def kernel(
    sizes,
    rhs, flux_in, mats, coef, perm, table, near, shift, blocks,
    sol_out, flux_out,
    bl, res, dirn, sol, fin, inv, fout,
    ax_send, ax_recv, co_send, co_recv,
    traces, resp, part_send, part_recv, harm, acc,
    in_sem, bl_sem, out_sem, fo_sem,
    axs_sem, axr_sem, cos_sem, cor_sem,
    raws_sem, rawr_sem, ps_sem, pr_sem, hs_sem, hr_sem,
):
    exc, depth, axial, pts, nv, ns, nmat = sizes
    rows = depth * axial
    chunks = exc // CHUNK
    per_half = chunks // HALVES
    eh = exc // HALVES
    crow = CHUNK * rows
    groups = ns // GROUP
    steps = SWEEPS - 1
    v = lax.axis_index("vol")
    s = lax.axis_index("sec")
    up, down = lax.rem(v + 1, nv), lax.rem(v + nv - 1, nv)
    right, left = lax.rem(s + 1, ns), lax.rem(s + ns - 1, ns)
    low = lax.rem(s, GROUP)
    grp = s // GROUP
    mate2 = s + 2 - 4 * lax.rem(s // 2, 2)
    mate1 = s + 1 - 2 * lax.rem(s, 2)
    low2 = lax.rem(mate2, GROUP)

    load = []
    flux_load = pltpu.make_async_copy(flux_in, fin, in_sem.at[chunks])
    flux_load.start()
    for c in range(chunks):
        cp = pltpu.make_async_copy(
            rhs.at[pl.ds(c * crow, crow)], res.at[pl.ds(c * crow, crow)], in_sem.at[c]
        )
        cp.start()
        load.append(cp)
    kv = axial * pts
    bl_load = pltpu.make_async_copy(blocks, bl, bl_sem)
    bl_load.start()

    barrier = pltpu.get_barrier_semaphore()
    greet = [(lax.rem(v + k, nv), s) for k in range(1, nv)]
    greet += [(v, right), (v, left), (v, mate1), (v, mate2)]
    greet += [(v, lax.rem(grp + k, groups) * GROUP + low) for k in range(1, groups)]
    for dev in greet:
        pl.semaphore_signal(barrier, inc=1, device_id=dev, device_id_type=MESH)

    sigma = jnp.zeros((rows, pts), F32)
    ids = mats[...]
    for m in range(nmat):
        sigma = jnp.where(ids == m, coef[m], sigma)
    inv[...] = 1.0 / (6.0 + sigma)

    def remote(src, dst, ssem, rsem, dev):
        return pltpu.make_async_remote_copy(
            src_ref=src, dst_ref=dst, send_sem=ssem, recv_sem=rsem,
            device_id=dev, device_id_type=MESH,
        )

    pending = []
    row2 = lax.broadcasted_iota(jnp.int32, (2 * CHUNK, pts), 0)
    lane2 = lax.broadcasted_iota(jnp.int32, (2 * CHUNK, pts), 1)

    def picker(e, first, second):
        hit = ((row2 == e) & (lane2 == first)) | ((row2 == e + CHUNK) & (lane2 == second))
        return jnp.where(hit, 1.0, 0.0).astype(BF16)

    def pack(e, xb):
        return lax.dot_general(
            picker(e, pts - 1, 0), xb, (((1,), (1,)), ((), ())), preferred_element_type=F32
        )

    halo = {}

    def send_halo(k, c, packed):
        base = c * crow
        n = CHUNK * depth
        ax_send[k, c, 0] = dirn[pl.ds(base + axial - 1, n, stride=axial), :].astype(BF16)
        ax_send[k, c, 1] = dirn[pl.ds(base, n, stride=axial), :].astype(BF16)
        co_send[k, c, 0] = packed[:CHUNK].astype(BF16)
        co_send[k, c, 1] = packed[CHUNK:].astype(BF16)
        cps = []
        for i, (vd, sd) in enumerate(((up, right), (down, left))):
            cps.append(remote(ax_send.at[k, c, i], ax_recv.at[k, c, i],
                              axs_sem.at[k, c, i], axr_sem.at[k, c, i], (vd, s)))
            cps.append(remote(co_send.at[k, c, i], co_recv.at[k, c, i],
                              cos_sem.at[k, c, i], cor_sem.at[k, c, i], (v, sd)))
        for cp in cps:
            cp.start()
        halo[k, c] = cps

    flux_load.wait()
    waited = False
    for c in range(chunks):
        load[c].wait()

        def first(e, packed, c=c):
            at = pl.multiple_of(c * crow + e * rows, rows)
            top = pl.ds(at + (depth - 1) * axial, axial)
            fat = pl.multiple_of((c * CHUNK + e) * axial, axial)
            res[top, :] = res[top, :] + fin[pl.ds(fat, axial), :]
            here = pl.ds(at, rows)
            x = res[here, :] * inv[...]
            res[here, :] = x
            x = x / center
            dirn[here, :] = x
            sol[here, :] = x
            return packed + pack(e, x.astype(BF16))

        packed = lax.fori_loop(0, CHUNK, first, jnp.zeros((2 * CHUNK, rows), F32))
        if not waited:
            pl.semaphore_wait(barrier, len(greet))
            waited = True
        send_halo(0, c, packed)

    sigma_one = center / radius
    ratios = [1.0 / sigma_one]
    for _ in range(steps):
        ratios.append(1.0 / (2.0 * sigma_one - ratios[-1]))

    outs = []

    def sweep(k, c):
        for cp in halo[k, c]:
            cp.wait_recv()
        pending.extend(halo[k, c])
        a = ratios[k + 1] * ratios[k]
        b = 2.0 * ratios[k + 1] / radius
        cols = jnp.concatenate(
            [co_recv[k, c, 0].astype(F32), co_recv[k, c, 1].astype(F32)], axis=0
        ).T.astype(BF16)
        last = k + 1 == steps

        def pair(q, packed):
            hrow = pl.ds(pl.multiple_of(q * 2 * depth, 2 * depth), 2 * depth)
            lo = ax_recv[k, c, 0, hrow, :]
            hi = ax_recv[k, c, 1, hrow, :]
            for j in range(2):
                e = q * 2 + j
                here = pl.ds(pl.multiple_of(c * crow + e * rows, rows), rows)
                x = dirn[here, :]
                xb = x.astype(BF16)
                tot = jnp.dot(near[j], jnp.concatenate([xb, lo, hi], axis=0),
                              preferred_element_type=F32)
                tot = tot + jnp.dot(
                    jnp.concatenate([xb, cols], axis=1),
                    jnp.concatenate([shift[...], picker(e, 0, pts - 1)], axis=0),
                    preferred_element_type=F32)
                r = res[here, :] - x + inv[...] * tot
                y = a * x + b * r
                sol[here, :] = sol[here, :] + y
                if not last:
                    res[here, :] = r
                    dirn[here, :] = y
                    packed = packed + pack(e, y.astype(BF16))
            return packed

        packed = lax.fori_loop(0, CHUNK // 2, pair, jnp.zeros((2 * CHUNK, rows), F32))
        if not last:
            send_halo(k + 1, c, packed)
        else:
            cp = pltpu.make_async_copy(
                sol.at[pl.ds(c * crow, crow)], sol_out.at[pl.ds(c * crow, crow)], out_sem.at[c]
            )
            cp.start()
            outs.append(cp)
            h, off = c // per_half, (c % per_half) * CHUNK
            for z in range(axial):
                got = sol[pl.ds(c * crow + (depth - 1) * axial + z, CHUNK, stride=rows), :]
                traces[h, low, z, off:off + CHUNK, :] = got.astype(BF16)

    def weight(way, target, member):
        if way == 0:
            return table[perm[target], member]
        return table[perm[member], target]

    raw = (traces, resp)
    state = {}

    def mix(way, h, target, finish):
        ws = [weight(way, target, grp * GROUP + m) for m in range(GROUP)]

        def one(z, carry):
            total = ws[0] * raw[way][h, 0, z].astype(F32)
            for m in range(1, GROUP):
                total = total + ws[m] * raw[way][h, m, z].astype(F32)
            finish(z, total)
            return carry

        lax.fori_loop(0, axial, one, 0)

    def raw_copy(way, h, slot, i, dev):
        ref = raw[way].at[h, slot]
        return remote(ref, ref, raws_sem.at[way, h, i], rawr_sem.at[way, h, i], dev)

    def fold1(way, h):
        cp = raw_copy(way, h, low, 0, (v, mate2))
        cq = raw_copy(way, h, low, 1, (v, mate1))
        cp.start()
        cq.start()
        state[way, h] = [cp, cq]

    def fold2(way, h):
        state[way, h][0].wait_recv()
        cr = raw_copy(way, h, low2, 2, (v, mate1))
        cr.start()
        state[way, h].append(cr)

    def fold3(way, h):
        state[way, h][1].wait_recv()
        state[way, h][2].wait_recv()
        pending.extend(state[way, h])
        state[way, h] = []
        for k in range(1, groups):
            target = lax.rem(grp + k, groups) * GROUP + low

            def put(z, total, k=k):
                part_send[way, h, k - 1, z] = total.astype(BF16)

            mix(way, h, target, put)
            cp = remote(part_send.at[way, h, k - 1], part_recv.at[way, h, k - 1],
                        ps_sem.at[way, h, k - 1], pr_sem.at[way, h, k - 1], (v, target))
            cp.start()
            state[way, h].append(cp)

    def fold_end(way, h, put):
        for cp in state[way, h]:
            cp.wait_recv()
        pending.extend(state[way, h])

        def finish(z, total):
            for k in range(1, groups):
                total = total + part_recv[way, h, k - 1, z].astype(F32)
            put(z, total)

        mix(way, h, s, finish)

    gathers = {}

    def gather(h):
        def put(z, total):
            harm[h, v, z] = total.astype(BF16)

        fold_end(0, h, put)
        cps = []
        for k in range(1, nv):
            cp = remote(harm.at[h, v], harm.at[h, v], hs_sem.at[h, k - 1], hr_sem.at[h, k - 1],
                        (lax.rem(v + k, nv), s))
            cp.start()
            cps.append(cp)
        gathers[h] = cps

    state["bl"] = False

    def apply(h, k):
        if not state["bl"]:
            bl_load.wait()
            state["bl"] = True
        if k > 0:
            gathers[h][k - 1].wait_recv()
            pending.append(gathers[h][k - 1])
        src = lax.rem(v + nv - k, nv)
        lhs = jnp.concatenate([harm[h, src, z] for z in range(axial)], axis=1)
        zt = min(4, axial)
        krow = pl.ds(pl.multiple_of(src * kv, kv), kv)

        def tile(t, carry):
            col = pl.ds(pl.multiple_of(t * zt * pts, zt * pts), zt * pts)
            got = jnp.dot(lhs, bl[krow, col], preferred_element_type=F32)
            for i in range(zt):
                z = t * zt + i
                piece = got[:, i * pts:(i + 1) * pts]
                if k > 0:
                    piece = piece + acc[z]
                if k + 1 < nv:
                    acc[z] = piece
                else:
                    resp[h, low, z] = piece.astype(BF16)
            return carry

        lax.fori_loop(0, axial // zt, tile, 0)

    def finish_flux(h):
        def put(z, total):
            fout[pl.ds(h * eh * axial + z, eh, stride=axial), :] = total

        fold_end(1, h, put)
        n = eh * axial
        cp = pltpu.make_async_copy(
            fout.at[pl.ds(h * n, n)], flux_out.at[pl.ds(h * n, n)], fo_sem.at[h]
        )
        cp.start()
        outs.append(cp)

    def sweeps(h, k):
        for c in range(h * per_half, (h + 1) * per_half):
            sweep(k, c)

    def run_apply(h, lo, hi):
        for k in range(lo, hi):
            apply(h, k)

    cut = [nv * i // 4 for i in range(5)]
    for k in range(steps):
        sweeps(0, k)
    fold1(0, 0)
    sweeps(1, 0)
    fold2(0, 0)
    sweeps(1, 1)
    fold3(0, 0)
    sweeps(1, 2)
    fold1(0, 1)
    gather(0)
    run_apply(0, cut[0], cut[1])
    fold2(0, 1)
    run_apply(0, cut[1], cut[2])
    fold3(0, 1)
    run_apply(0, cut[2], cut[3])
    gather(1)
    run_apply(0, cut[3], cut[4])
    fold1(1, 0)
    run_apply(1, cut[0], cut[1])
    fold2(1, 0)
    run_apply(1, cut[1], cut[2])
    fold3(1, 0)
    run_apply(1, cut[2], cut[4])
    fold1(1, 1)
    finish_flux(0)
    fold2(1, 1)
    fold3(1, 1)
    finish_flux(1)

    for cp in pending:
        cp.wait_send()
    for cp in outs:
        cp.wait()


def per_device(ns, nv, rhs, flux_in, materials, mat_coef, owner_perm, blocks):
    exc, depth, axial, pts = rhs.shape
    rows = depth * axial
    order, width = blocks.shape[1:]
    chunks = exc // CHUNK
    eh = exc // HALVES
    groups = ns // GROUP
    steps = SWEEPS - 1
    near, shift = neighbour_matrices(depth, axial, pts)
    sizes = (exc, depth, axial, pts, nv, ns, mat_coef.shape[0])
    vm = pl.BlockSpec(memory_space=pltpu.VMEM)
    sm = pl.BlockSpec(memory_space=pltpu.SMEM)
    hb = pl.BlockSpec(memory_space=pl.ANY)
    dma = pltpu.SemaphoreType.DMA
    item = (axial, eh, pts)
    sol, flux = pl.pallas_call(
        functools.partial(kernel, sizes),
        out_shape=(
            jax.ShapeDtypeStruct((exc * rows, pts), F32),
            jax.ShapeDtypeStruct((exc * axial, pts), F32),
        ),
        in_specs=[hb, hb, vm, sm, sm, sm, vm, vm, hb],
        out_specs=(hb, hb),
        scratch_shapes=[
            pltpu.VMEM((order, width), BF16),
            pltpu.VMEM((exc * rows, pts), F32),
            pltpu.VMEM((exc * rows, pts), F32),
            pltpu.VMEM((exc * rows, pts), F32),
            pltpu.VMEM((exc * axial, pts), F32),
            pltpu.VMEM((rows, pts), F32),
            pltpu.VMEM((exc * axial, pts), F32),
            pltpu.VMEM((steps, chunks, 2, CHUNK * depth, pts), BF16),
            pltpu.VMEM((steps, chunks, 2, CHUNK * depth, pts), BF16),
            pltpu.VMEM((steps, chunks, 2, CHUNK, rows), BF16),
            pltpu.VMEM((steps, chunks, 2, CHUNK, rows), BF16),
            pltpu.VMEM((HALVES, GROUP) + item, BF16),
            pltpu.VMEM((HALVES, GROUP) + item, BF16),
            pltpu.VMEM((2, HALVES, groups - 1) + item, BF16),
            pltpu.VMEM((2, HALVES, groups - 1) + item, BF16),
            pltpu.VMEM((HALVES, nv) + item, BF16),
            pltpu.VMEM(item, F32),
            dma((chunks + 1,)), dma, dma((chunks,)), dma((HALVES,)),
            dma((steps, chunks, 2)), dma((steps, chunks, 2)),
            dma((steps, chunks, 2)), dma((steps, chunks, 2)),
            dma((2, HALVES, 3)), dma((2, HALVES, 3)),
            dma((2, HALVES, groups - 1)), dma((2, HALVES, groups - 1)),
            dma((HALVES, nv - 1)), dma((HALVES, nv - 1)),
        ],
        compiler_params=pltpu.CompilerParams(
            collective_id=0, has_side_effects=True, vmem_limit_bytes=60 * 2**20
        ),
        cost_estimate=pl.CostEstimate(
            flops=2 * exc * order * width, bytes_accessed=2 * order * width, transcendentals=0
        ),
    )(
        rhs.reshape(exc * rows, pts),
        flux_in.reshape(exc * axial, pts),
        materials.reshape(rows, pts),
        mat_coef,
        owner_perm,
        jnp.asarray(basis_table(ns)),
        near,
        shift,
        blocks[0],
    )
    return sol.reshape(rhs.shape), flux.reshape(flux_in.shape)


def solution(mesh):
    return jax.shard_map(
        functools.partial(per_device, mesh.shape["sec"], mesh.shape["vol"]),
        mesh=mesh,
        in_specs=(
            P(None, None, "vol", "sec"),
            P(None, "vol", "sec"),
            P(None, "vol", "sec"),
            P(),
            P(),
            P("sec", None, "vol"),
        ),
        out_specs=(P(None, None, "vol", "sec"), P(None, "vol", "sec")),
        check_vma=False,
    )
```

```python
import functools
import math

import jax
import jax.numpy as jnp
import numpy as np
from jax import lax
from jax.experimental import pallas as pl
from jax.experimental.pallas import tpu as pltpu
from jax.sharding import PartitionSpec as P

SWEEPS = 4
HALVES = 2
CHUNK = 16
GROUP = 4
MESH = pl.DeviceIdType.MESH
F32, BF16 = jnp.float32, jnp.bfloat16

center = 1.0
radius = 0.93


def basis_table(count):
    harm = np.arange(count)[:, None]
    sect = np.arange(count)[None, :]
    mid = count // 2
    wave = np.where(harm <= mid, harm, harm - mid)
    phase = 2.0 * np.pi * (wave * sect % count) / count
    value = np.where(harm <= mid, np.cos(phase), np.sin(phase))
    ends = (harm == 0) | (harm == mid)
    return (value * np.where(ends, math.sqrt(1.0 / count), math.sqrt(2.0 / count))).astype(np.float32)


def neighbour_matrices(depth, axial, pts):
    rows = depth * axial
    d, z = np.divmod(np.arange(rows), axial)
    same_d = d[:, None] == d[None, :]
    same_z = z[:, None] == z[None, :]
    near = (same_d & (abs(z[:, None] - z[None, :]) == 1)) | (
        same_z & (abs(d[:, None] - d[None, :]) == 1)
    )
    out = np.zeros((2, rows, rows + 4 * depth), np.float32)
    out[:, :, :rows] = near
    for j in range(2):
        for layer in range(depth):
            out[j, layer * axial, rows + j * depth + layer] = 1.0
            out[j, layer * axial + axial - 1, rows + 2 * depth + j * depth + layer] = 1.0
    p = np.arange(pts)
    shift = (abs(p[:, None] - p[None, :]) == 1).astype(np.float32)
    sides = np.zeros((2 * CHUNK, pts), np.float32)
    sides[:CHUNK, 0] = 1.0
    sides[CHUNK:, pts - 1] = 1.0
    edges = np.zeros((pts, pts), np.float32)
    edges[pts - 1, :CHUNK] = 1.0
    edges[0, CHUNK:2 * CHUNK] = 1.0
    shift = np.concatenate([shift, sides], axis=0)
    return jnp.asarray(out, BF16), jnp.asarray(shift, BF16), jnp.asarray(edges, BF16)


def kernel(
    sizes,
    rhs, flux_in, mats, coef, perm, table, near, shift, edges, blocks,
    sol_out, flux_out,
    bl, res, dirn, sol, fin, inv, fout,
    ax_send, ax_recv, co_send, co_recv,
    traces, resp, part_send, part_recv, harm, acc,
    in_sem, bl_sem, out_sem, fo_sem,
    axs_sem, axr_sem, cos_sem, cor_sem,
    raws_sem, rawr_sem, ps_sem, pr_sem, hs_sem, hr_sem,
):
    exc, depth, axial, pts, nv, ns, nmat = sizes
    rows = depth * axial
    chunks = exc // CHUNK
    per_half = chunks // HALVES
    eh = exc // HALVES
    crow = CHUNK * rows
    groups = ns // GROUP
    steps = SWEEPS - 1
    v = lax.axis_index("vol")
    s = lax.axis_index("sec")
    up, down = lax.rem(v + 1, nv), lax.rem(v + nv - 1, nv)
    right, left = lax.rem(s + 1, ns), lax.rem(s + ns - 1, ns)
    low = lax.rem(s, GROUP)
    grp = s // GROUP
    mate2 = s + 2 - 4 * lax.rem(s // 2, 2)
    mate1 = s + 1 - 2 * lax.rem(s, 2)
    low2 = lax.rem(mate2, GROUP)

    load = []
    flux_load = pltpu.make_async_copy(flux_in, fin, in_sem.at[chunks])
    flux_load.start()
    for c in range(chunks):
        cp = pltpu.make_async_copy(
            rhs.at[pl.ds(c * crow, crow)], res.at[pl.ds(c * crow, crow)], in_sem.at[c]
        )
        cp.start()
        load.append(cp)
    kv = axial * pts
    bl_load = pltpu.make_async_copy(blocks, bl, bl_sem)
    bl_load.start()

    barrier = pltpu.get_barrier_semaphore()
    greet = [(lax.rem(v + k, nv), s) for k in range(1, nv)]
    greet += [(v, right), (v, left), (v, mate1), (v, mate2)]
    greet += [(v, lax.rem(grp + k, groups) * GROUP + low) for k in range(1, groups)]
    for dev in greet:
        pl.semaphore_signal(barrier, inc=1, device_id=dev, device_id_type=MESH)

    sigma = jnp.zeros((rows, pts), F32)
    ids = mats[...]
    for m in range(nmat):
        sigma = jnp.where(ids == m, coef[m], sigma)
    inv[...] = 1.0 / (6.0 + sigma)

    def remote(src, dst, ssem, rsem, dev):
        return pltpu.make_async_remote_copy(
            src_ref=src, dst_ref=dst, send_sem=ssem, recv_sem=rsem,
            device_id=dev, device_id_type=MESH,
        )

    pending = []
    lane = lax.broadcasted_iota(jnp.int32, (rows, pts), 1)
    side = lax.broadcasted_iota(jnp.int32, (rows, 2 * CHUNK), 1)

    def pack(e, xb, packed):
        both = jnp.dot(xb, edges[...], preferred_element_type=F32)
        return jnp.where((lane == e) | (lane == e + CHUNK), both, packed)

    halo = {}

    def send_halo(k, c, packed):
        base = c * crow
        n = CHUNK * depth
        ax_send[k, c, 0] = dirn[pl.ds(base + axial - 1, n, stride=axial), :].astype(BF16)
        ax_send[k, c, 1] = dirn[pl.ds(base, n, stride=axial), :].astype(BF16)
        turned = packed.T
        co_send[k, c, 0] = turned[:CHUNK].astype(BF16)
        co_send[k, c, 1] = turned[CHUNK:2 * CHUNK].astype(BF16)
        cps = []
        for i, (vd, sd) in enumerate(((up, right), (down, left))):
            cps.append(remote(ax_send.at[k, c, i], ax_recv.at[k, c, i],
                              axs_sem.at[k, c, i], axr_sem.at[k, c, i], (vd, s)))
            cps.append(remote(co_send.at[k, c, i], co_recv.at[k, c, i],
                              cos_sem.at[k, c, i], cor_sem.at[k, c, i], (v, sd)))
        for cp in cps:
            cp.start()
        halo[k, c] = cps

    flux_load.wait()
    waited = False
    for c in range(chunks):
        load[c].wait()

        def first(e, packed, c=c):
            at = pl.multiple_of(c * crow + e * rows, rows)
            top = pl.ds(at + (depth - 1) * axial, axial)
            fat = pl.multiple_of((c * CHUNK + e) * axial, axial)
            res[top, :] = res[top, :] + fin[pl.ds(fat, axial), :]
            here = pl.ds(at, rows)
            x = res[here, :] * inv[...]
            res[here, :] = x
            x = x / center
            dirn[here, :] = x
            sol[here, :] = x
            return pack(e, x.astype(BF16), packed)

        packed = lax.fori_loop(0, CHUNK, first, jnp.zeros((rows, pts), F32))
        if not waited:
            pl.semaphore_wait(barrier, len(greet))
            waited = True
        send_halo(0, c, packed)

    sigma_one = center / radius
    ratios = [1.0 / sigma_one]
    for _ in range(steps):
        ratios.append(1.0 / (2.0 * sigma_one - ratios[-1]))

    outs = []

    def sweep(k, c):
        for cp in halo[k, c]:
            cp.wait_recv()
        pending.extend(halo[k, c])
        a = ratios[k + 1] * ratios[k]
        b = 2.0 * ratios[k + 1] / radius
        cols = jnp.concatenate(
            [co_recv[k, c, 0].astype(F32), co_recv[k, c, 1].astype(F32)], axis=0
        ).T
        last = k + 1 == steps

        def pair(q, packed):
            hrow = pl.ds(pl.multiple_of(q * 2 * depth, 2 * depth), 2 * depth)
            lo = ax_recv[k, c, 0, hrow, :]
            hi = ax_recv[k, c, 1, hrow, :]
            for j in range(2):
                e = q * 2 + j
                here = pl.ds(pl.multiple_of(c * crow + e * rows, rows), rows)
                x = dirn[here, :]
                xb = x.astype(BF16)
                tot = jnp.dot(near[j], jnp.concatenate([xb, lo, hi], axis=0),
                              preferred_element_type=F32)
                own = jnp.where((side == e) | (side == e + CHUNK), cols, 0.0).astype(BF16)
                tot = tot + jnp.dot(jnp.concatenate([xb, own], axis=1), shift[...],
                                    preferred_element_type=F32)
                r = res[here, :] - x + inv[...] * tot
                y = a * x + b * r
                sol[here, :] = sol[here, :] + y
                if not last:
                    res[here, :] = r
                    dirn[here, :] = y
                    packed = pack(e, y.astype(BF16), packed)
            return packed

        packed = lax.fori_loop(0, CHUNK // 2, pair, jnp.zeros((rows, pts), F32))
        if not last:
            send_halo(k + 1, c, packed)
        else:
            cp = pltpu.make_async_copy(
                sol.at[pl.ds(c * crow, crow)], sol_out.at[pl.ds(c * crow, crow)], out_sem.at[c]
            )
            cp.start()
            outs.append(cp)
            h, off = c // per_half, (c % per_half) * CHUNK
            for z in range(axial):
                got = sol[pl.ds(c * crow + (depth - 1) * axial + z, CHUNK, stride=rows), :]
                traces[h, low, z, off:off + CHUNK, :] = got.astype(BF16)

    def weight(way, target, member):
        if way == 0:
            return table[perm[target], member]
        return table[perm[member], target]

    raw = (traces, resp)
    state = {}

    def mix(way, h, target, finish):
        ws = [weight(way, target, grp * GROUP + m) for m in range(GROUP)]

        def one(z, carry):
            total = ws[0] * raw[way][h, 0, z].astype(F32)
            for m in range(1, GROUP):
                total = total + ws[m] * raw[way][h, m, z].astype(F32)
            finish(z, total)
            return carry

        lax.fori_loop(0, axial, one, 0)

    def raw_copy(way, h, slot, i, dev):
        ref = raw[way].at[h, slot]
        return remote(ref, ref, raws_sem.at[way, h, i], rawr_sem.at[way, h, i], dev)

    def fold1(way, h):
        cp = raw_copy(way, h, low, 0, (v, mate2))
        cq = raw_copy(way, h, low, 1, (v, mate1))
        cp.start()
        cq.start()
        state[way, h] = [cp, cq]

    def fold2(way, h):
        state[way, h][0].wait_recv()
        cr = raw_copy(way, h, low2, 2, (v, mate1))
        cr.start()
        state[way, h].append(cr)

    def fold3(way, h):
        state[way, h][1].wait_recv()
        state[way, h][2].wait_recv()
        pending.extend(state[way, h])
        state[way, h] = []
        for k in range(1, groups):
            target = lax.rem(grp + k, groups) * GROUP + low

            def put(z, total, k=k):
                part_send[way, h, k - 1, z] = total.astype(BF16)

            mix(way, h, target, put)
            cp = remote(part_send.at[way, h, k - 1], part_recv.at[way, h, k - 1],
                        ps_sem.at[way, h, k - 1], pr_sem.at[way, h, k - 1], (v, target))
            cp.start()
            state[way, h].append(cp)

    def fold_end(way, h, put):
        for cp in state[way, h]:
            cp.wait_recv()
        pending.extend(state[way, h])

        def finish(z, total):
            for k in range(1, groups):
                total = total + part_recv[way, h, k - 1, z].astype(F32)
            put(z, total)

        mix(way, h, s, finish)

    gathers = {}

    def gather(h):
        def put(z, total):
            harm[h, v, z] = total.astype(BF16)

        fold_end(0, h, put)
        cps = []
        for k in range(1, nv):
            cp = remote(harm.at[h, v], harm.at[h, v], hs_sem.at[h, k - 1], hr_sem.at[h, k - 1],
                        (lax.rem(v + k, nv), s))
            cp.start()
            cps.append(cp)
        gathers[h] = cps

    state["bl"] = False

    def apply(h, k):
        if not state["bl"]:
            bl_load.wait()
            state["bl"] = True
        if k > 0:
            gathers[h][k - 1].wait_recv()
            pending.append(gathers[h][k - 1])
        src = lax.rem(v + nv - k, nv)
        lhs = jnp.concatenate([harm[h, src, z] for z in range(axial)], axis=1)
        zt = min(4, axial)
        krow = pl.ds(pl.multiple_of(src * kv, kv), kv)

        def tile(t, carry):
            col = pl.ds(pl.multiple_of(t * zt * pts, zt * pts), zt * pts)
            got = jnp.dot(lhs, bl[krow, col], preferred_element_type=F32)
            for i in range(zt):
                z = t * zt + i
                piece = got[:, i * pts:(i + 1) * pts]
                if k > 0:
                    piece = piece + acc[z]
                if k + 1 < nv:
                    acc[z] = piece
                else:
                    resp[h, low, z] = piece.astype(BF16)
            return carry

        lax.fori_loop(0, axial // zt, tile, 0)

    def finish_flux(h):
        def put(z, total):
            fout[pl.ds(h * eh * axial + z, eh, stride=axial), :] = total

        fold_end(1, h, put)
        n = eh * axial
        cp = pltpu.make_async_copy(
            fout.at[pl.ds(h * n, n)], flux_out.at[pl.ds(h * n, n)], fo_sem.at[h]
        )
        cp.start()
        outs.append(cp)

    def sweeps(h, k):
        for c in range(h * per_half, (h + 1) * per_half):
            sweep(k, c)

    def run_apply(h, lo, hi):
        for k in range(lo, hi):
            apply(h, k)

    cut = [nv * i // 4 for i in range(5)]
    for k in range(steps):
        sweeps(0, k)
    fold1(0, 0)
    sweeps(1, 0)
    fold2(0, 0)
    sweeps(1, 1)
    fold3(0, 0)
    sweeps(1, 2)
    fold1(0, 1)
    gather(0)
    run_apply(0, cut[0], cut[1])
    fold2(0, 1)
    run_apply(0, cut[1], cut[2])
    fold3(0, 1)
    run_apply(0, cut[2], cut[3])
    gather(1)
    run_apply(0, cut[3], cut[4])
    fold1(1, 0)
    run_apply(1, cut[0], cut[1])
    fold2(1, 0)
    run_apply(1, cut[1], cut[2])
    fold3(1, 0)
    run_apply(1, cut[2], cut[4])
    fold1(1, 1)
    finish_flux(0)
    fold2(1, 1)
    fold3(1, 1)
    finish_flux(1)

    for cp in pending:
        cp.wait_send()
    for cp in outs:
        cp.wait()


def per_device(ns, nv, rhs, flux_in, materials, mat_coef, owner_perm, blocks):
    exc, depth, axial, pts = rhs.shape
    rows = depth * axial
    order, width = blocks.shape[1:]
    chunks = exc // CHUNK
    eh = exc // HALVES
    groups = ns // GROUP
    steps = SWEEPS - 1
    near, shift, edges = neighbour_matrices(depth, axial, pts)
    sizes = (exc, depth, axial, pts, nv, ns, mat_coef.shape[0])
    vm = pl.BlockSpec(memory_space=pltpu.VMEM)
    sm = pl.BlockSpec(memory_space=pltpu.SMEM)
    hb = pl.BlockSpec(memory_space=pl.ANY)
    dma = pltpu.SemaphoreType.DMA
    item = (axial, eh, pts)
    sol, flux = pl.pallas_call(
        functools.partial(kernel, sizes),
        out_shape=(
            jax.ShapeDtypeStruct((exc * rows, pts), F32),
            jax.ShapeDtypeStruct((exc * axial, pts), F32),
        ),
        in_specs=[hb, hb, vm, sm, sm, sm, vm, vm, vm, hb],
        out_specs=(hb, hb),
        scratch_shapes=[
            pltpu.VMEM((order, width), BF16),
            pltpu.VMEM((exc * rows, pts), F32),
            pltpu.VMEM((exc * rows, pts), F32),
            pltpu.VMEM((exc * rows, pts), F32),
            pltpu.VMEM((exc * axial, pts), F32),
            pltpu.VMEM((rows, pts), F32),
            pltpu.VMEM((exc * axial, pts), F32),
            pltpu.VMEM((steps, chunks, 2, CHUNK * depth, pts), BF16),
            pltpu.VMEM((steps, chunks, 2, CHUNK * depth, pts), BF16),
            pltpu.VMEM((steps, chunks, 2, CHUNK, rows), BF16),
            pltpu.VMEM((steps, chunks, 2, CHUNK, rows), BF16),
            pltpu.VMEM((HALVES, GROUP) + item, BF16),
            pltpu.VMEM((HALVES, GROUP) + item, BF16),
            pltpu.VMEM((2, HALVES, groups - 1) + item, BF16),
            pltpu.VMEM((2, HALVES, groups - 1) + item, BF16),
            pltpu.VMEM((HALVES, nv) + item, BF16),
            pltpu.VMEM(item, F32),
            dma((chunks + 1,)), dma, dma((chunks,)), dma((HALVES,)),
            dma((steps, chunks, 2)), dma((steps, chunks, 2)),
            dma((steps, chunks, 2)), dma((steps, chunks, 2)),
            dma((2, HALVES, 3)), dma((2, HALVES, 3)),
            dma((2, HALVES, groups - 1)), dma((2, HALVES, groups - 1)),
            dma((HALVES, nv - 1)), dma((HALVES, nv - 1)),
        ],
        compiler_params=pltpu.CompilerParams(
            collective_id=0, has_side_effects=True, vmem_limit_bytes=60 * 2**20
        ),
        cost_estimate=pl.CostEstimate(
            flops=2 * exc * order * width, bytes_accessed=2 * order * width, transcendentals=0
        ),
    )(
        rhs.reshape(exc * rows, pts),
        flux_in.reshape(exc * axial, pts),
        materials.reshape(rows, pts),
        mat_coef,
        owner_perm,
        jnp.asarray(basis_table(ns)),
        near,
        shift,
        edges,
        blocks[0],
    )
    return sol.reshape(rhs.shape), flux.reshape(flux_in.shape)


def solution(mesh):
    return jax.shard_map(
        functools.partial(per_device, mesh.shape["sec"], mesh.shape["vol"]),
        mesh=mesh,
        in_specs=(
            P(None, None, "vol", "sec"),
            P(None, "vol", "sec"),
            P(None, "vol", "sec"),
            P(),
            P(),
            P("sec", None, "vol"),
        ),
        out_specs=(P(None, None, "vol", "sec"), P(None, "vol", "sec")),
        check_vma=False,
    )
```
